32 devices in a mesh: flow: 8 (over z, x), cross: 4 (over y, core).
Axes of the slice: x: 2, y: 2, z: 4, core: 2. Of those that a mesh axis runs over, the one named last changes fastest.
Arguments:
- particles: float32 [1536, 8, 128], P(('flow', 'cross')), may hold values from -1.5 to 48, as said below
- counts: int32 [1536], P(('flow', 'cross')), may hold values from 32 to 128, as said below
- pairs: int32 [1536, 45], P(('flow', 'cross')), may hold values from 0 to 959, as said below
Outputs:
- rates: float32 [1536, 4, 128], P(('flow', 'cross'))
The draws below stay inside these ranges and needn't reach their ends.
Inputs may be any that keep to these rules, and one draw needn't show every extreme that they name: `particles`: each block holds one cell of 1 x 2 x 2 (cells have y index in 0 to 7 and z index in 0 to 23); which cell a block holds follows one order, the same in every slab; positions lie inside their cell; density between 0.9 and 1.1, positive masses. `counts`: some block is full. `pairs`: the codes of a block name the blocks of its own cell and of its neighbour cells within one cell across (periodic) and two slabs along the flow.
All inputs are finite; a program needn't handle non-finite values.
Results may differ from the reference program's by a relative error of at most 0.0003.
Values sent between devices are 32-bit elements; how exact they have to be, the bound alone decides.
A program may use at most 64 MiB of HBM per device.

```python
import math
import jax
import jax.numpy as jnp
from jax import lax

BS = 128
NB = 45
GY = 8
SLAB_BLK = 192
GZ = 24
SLABS = 8
BLOCKS_ALL = 1536


def cell_order(key):
    return jax.random.permutation(jax.random.fold_in(key, 101), SLAB_BLK).astype(jnp.int32)


def draw_pairs(key, part):
    order = cell_order(key)
    block_of_cell = jnp.argsort(order, stable=True).astype(jnp.int32)
    cell_y = order % GY
    cell_z = order // GY
    code_list = []
    for slab_rel in (-2, -1, 0, 1, 2):
        for step_y in (-1, 0, 1):
            for step_z in (-1, 0, 1):
                other_cell = jnp.mod(cell_y + step_y, GY) + GY * jnp.mod(cell_z + step_z, GZ)
                code_list.append((slab_rel + 2) * SLAB_BLK + block_of_cell[other_cell])
    codes = jnp.stack(code_list, axis=-1)
    return jnp.broadcast_to(codes[None], (SLABS, SLAB_BLK, NB)).reshape(BLOCKS_ALL, NB).astype(jnp.int32)


def draw_counts(key, part):
    values = jax.random.randint(jax.random.fold_in(key, 202), (BLOCKS_ALL,), BS // 4, BS + 1)
    chosen = jax.random.randint(jax.random.fold_in(key, 203), (), 0, BLOCKS_ALL)
    return jnp.where(jnp.arange(BLOCKS_ALL) == chosen, BS, values).astype(jnp.int32)


def draw_particles(key, part):
    order = cell_order(key)
    cells = order[jnp.arange(BLOCKS_ALL, dtype=jnp.int32) % SLAB_BLK]
    cell_y = (cells % GY).astype(jnp.float32)[:, None]
    cell_z = (cells // GY).astype(jnp.float32)[:, None]
    key_list = jax.random.split(jax.random.fold_in(key, 303), 8)
    shape = (BLOCKS_ALL, BS)
    pos_x = jax.random.uniform(key_list[0], shape, jnp.float32)
    pos_y = 2.0 * cell_y + 2.0 * jax.random.uniform(key_list[1], shape, jnp.float32)
    pos_z = 2.0 * cell_z + 2.0 * jax.random.uniform(key_list[2], shape, jnp.float32)
    vel_u = jnp.clip(0.5 * jax.random.normal(key_list[3], shape, jnp.float32), -1.5, 1.5)
    vel_v = jnp.clip(0.5 * jax.random.normal(key_list[4], shape, jnp.float32), -1.5, 1.5)
    vel_w = jnp.clip(0.5 * jax.random.normal(key_list[5], shape, jnp.float32), -1.5, 1.5)
    density = 0.9 + 0.2 * jax.random.uniform(key_list[6], shape, jnp.float32)
    mass = density * (6.4 / BS) * jnp.exp(jax.random.uniform(key_list[7], shape, jnp.float32, -0.3, 0.3))
    return jnp.stack([pos_x, pos_y, pos_z, vel_u, vel_v, vel_w, density, mass], axis=1).astype(jnp.float32)


def setup_inputs(seed: int = 0) -> dict:
    keys = jax.random.split(jax.random.key(seed), 4)
    return {
        "particles": draw_particles(jax.random.fold_in(keys[3], 71), 0),
        "counts": draw_counts(jax.random.fold_in(keys[3], 71), 0),
        "pairs": draw_pairs(jax.random.fold_in(keys[3], 71), 0),
    }


kernel_coef = 5.0 * 21.0 / (16.0 * math.pi)
eta_square = 0.01
sound_speed = 6.0
delta_coef = 0.1
visc_coef = 0.1

def wrap_gap(gap, width):
    return gap - width * jnp.floor(gap / width + 0.5)

def interact(target, target_count, sources, source_count, slab_gap, wide_y, wide_z):
    slot_ids = jnp.arange(target.shape[1], dtype=jnp.int32)
    target_live = (slot_ids < target_count).astype(jnp.float32)
    source_live = (slot_ids[None, :] < source_count[:, None]).astype(jnp.float32)

    def target_field(field):
        return target[field][None, :, None]

    def source_field(field):
        return sources[:, field][:, None, :]
    gap_x = target_field(0) - source_field(0) - slab_gap[:, None, None]
    gap_y = wrap_gap(target_field(1) - source_field(1), wide_y)
    gap_z = wrap_gap(target_field(2) - source_field(2), wide_z)
    dist_sq = gap_x * gap_x + gap_y * gap_y + gap_z * gap_z
    radius = jnp.sqrt(dist_sq + eta_square)
    kernel = kernel_coef * jnp.maximum(1.0 - 0.5 * radius, 0.0) ** 3
    volume = (sources[:, 7] / sources[:, 6] * source_live)[:, None, :]
    weight = volume * kernel
    rho_i = target_field(6)
    rho_j = source_field(6)
    closing = (target_field(3) - source_field(3)) * gap_x + (target_field(4) - source_field(4)) * gap_y + (target_field(5) - source_field(5)) * gap_z
    density_term = weight * (-rho_i * closing + 2.0 * delta_coef * sound_speed * (rho_j - rho_i) * dist_sq / (dist_sq + eta_square))
    drho = lax.optimization_barrier(jnp.sum(density_term, axis=(0, 2)))
    pressure_term = weight * (sound_speed * sound_speed * (rho_i - 1.0) + sound_speed * sound_speed * (rho_j - 1.0) - visc_coef * sound_speed * closing / (dist_sq + eta_square))
    accel_x = lax.optimization_barrier(jnp.sum(pressure_term * gap_x, axis=(0, 2))) / target[6]
    accel_y = lax.optimization_barrier(jnp.sum(pressure_term * gap_y, axis=(0, 2))) / target[6]
    accel_z = lax.optimization_barrier(jnp.sum(pressure_term * gap_z, axis=(0, 2))) / target[6]
    return jnp.stack([drho, accel_x, accel_y, accel_z]) * target_live[None, :]

def reference(particles, counts, pairs):

    def per_block(packed):
        target, target_count, pair_codes, block_id = packed
        slab_id = block_id // SLAB_BLK
        slab_rel = pair_codes // SLAB_BLK - 2
        source_ids = (jnp.mod(slab_id + slab_rel, SLABS) * SLAB_BLK + jnp.mod(pair_codes, SLAB_BLK)).astype(jnp.int32)
        sources = particles[source_ids]
        source_count = counts[source_ids]
        return interact(target, target_count, sources, source_count, slab_rel.astype(jnp.float32), 2.0 * GY, 2.0 * GZ)
    return lax.map(per_block, (particles, counts, pairs, jnp.arange(BLOCKS_ALL, dtype=jnp.int32)))
```

```python
import functools
import math

import jax
import jax.numpy as jnp
from jax import lax
from jax.experimental import pallas as pl
from jax.experimental.pallas import tpu as pltpu
from jax.sharding import PartitionSpec as P

GY = 8


kernel_coef = 5.0 * 21.0 / (16.0 * math.pi)
eta_square = 0.01
sound_speed = 6.0
delta_coef = 0.1
visc_coef = 0.1
slab_order = (-2, -1, 0, 1, 2)
wave = sound_speed * visc_coef
stiff = sound_speed / visc_coef
rows_step = 16
fields = 7


def passed_along(value, axis, steps):
    count = lax.axis_size(axis)
    pairs = [(source, (source + steps) % count) for source in range(count)]
    return lax.ppermute(value, axis, pairs)


def pair_kernel(per_block, wide_y, wide_z, codes, live_counts, source_counts, target, columns, lookup, out, packed, spread, totals):
    block = pl.program_id(0)
    slots = target.shape[2]
    lanes = lax.broadcasted_iota(jnp.int32, (8, slots), 1)
    row = lax.broadcasted_iota(jnp.int32, (8, slots), 0)
    wide = jnp.where(row == 1, wide_y, jnp.where(row == 2, wide_z, 0.0))
    inverse = jnp.where(row == 1, 1.0 / wide_y, jnp.where(row == 2, 1.0 / wide_z, 0.0))
    own = target[0]
    own_first = jnp.broadcast_to(own[:, 0:1], (8, slots)) * inverse + 0.5

    def pack(step, state):
        current, tile, start = state
        code = codes[block * per_block + step]
        count = source_counts[code]
        value = lookup[code]
        first = jnp.broadcast_to(value[:, 0:1], (8, slots))
        value = value + wide * jnp.floor(own_first - first * inverse)
        turned = pltpu.roll(value, start, 1)
        ahead = lanes >= start
        merged = jnp.where(ahead, turned, current)
        packed[tile] = merged
        end = start + count
        full = (end >= slots).astype(jnp.int32)
        keep = jnp.broadcast_to(full, (8, slots)) == 0
        rest = jnp.where(ahead, 0.0, turned)
        return jnp.where(keep, merged, rest), tile + full, end - full * slots

    empty = jnp.zeros((8, slots), jnp.float32)
    current, tile, start = lax.fori_loop(0, per_block, pack, (empty, jnp.int32(0), jnp.int32(0)), unroll=5)
    packed[tile] = current
    packed[tile + 1] = empty
    tiles = tile + (start > 0).astype(jnp.int32)

    for group in range(slots // 8):
        part = columns[0, group * 8:group * 8 + 8, :]
        for field in range(fields):
            spread[field, group * 8:group * 8 + 8, :] = jnp.broadcast_to(part[:, field:field + 1], (8, slots))

    live = live_counts[block]

    def per_rows(index, unused):
        first = pl.multiple_of(index * rows_step, rows_step)
        rows = pl.ds(first, rows_step)
        xi, yi, zi, ui, vi, wi, pi = [spread[field, rows, :] for field in range(fields)]

        def one_tile(place, sums):
            s_close, s_diff, s_damp, s_x, s_y, s_z = sums
            xj, yj, zj, uj, vj, wj, pj, volume = [packed[place, field:field + 1, :] for field in range(8)]
            gap_x = xi - xj
            gap_y = yi - yj
            gap_z = zi - zj
            shifted = (gap_x * gap_x + eta_square) + (gap_y * gap_y + gap_z * gap_z)
            inv = lax.rsqrt(shifted)
            bump = jnp.maximum(2.0 - shifted * inv, 0.0)
            weight = (bump * bump) * (bump * volume)
            closing = (ui - uj) * gap_x + (vi - vj) * gap_y + (wi - wj) * gap_z
            inv_sq = inv * inv
            diff = weight * (pj - pi)
            push = weight * ((pi + pj) - closing * inv_sq)
            return (
                s_close + weight * closing,
                s_diff + diff,
                s_damp + diff * inv_sq,
                s_x + push * gap_x,
                s_y + push * gap_y,
                s_z + push * gap_z,
            )

        def two_tiles(place, sums):
            return one_tile(2 * place + 1, one_tile(2 * place, sums))

        zero = jnp.zeros((rows_step, slots), jnp.float32)
        sums = lax.fori_loop(0, (tiles + 1) // 2, two_tiles, (zero,) * 6)
        totals[0, rows, :] = sums[0]
        totals[1, rows, :] = sums[1] - eta_square * sums[2]
        totals[2, rows, :] = sums[3]
        totals[3, rows, :] = sums[4]
        totals[4, rows, :] = sums[5]
        return unused

    lax.fori_loop(0, (live + rows_step - 1) // rows_step, per_rows, 0)

    ones = jnp.ones((8, slots), jnp.float32)

    def summed(which):
        return lax.dot_general(
            ones, totals[which], (((1,), (1,)), ((), ())),
            precision=lax.Precision.HIGHEST, preferred_element_type=jnp.float32,
        )[0:1]

    rho = own[6:7]
    scale = kernel_coef / 8.0
    drho = scale * (2.0 * delta_coef * sound_speed / stiff * summed(1) - rho * summed(0))
    over = (scale * wave) / rho
    alive = lanes[0:1] < live
    out[0, 0:1, :] = jnp.where(alive, drho, 0.0)
    for axis in range(3):
        out[0, axis + 1:axis + 2, :] = jnp.where(alive, over * summed(2 + axis), 0.0)


def per_device(particles, counts, pairs):
    blocks, width, slots = particles.shape
    slab_blk = blocks * lax.axis_size("cross")
    cells_z = slab_blk // GY
    per_block = pairs.shape[1]
    slot_ids = jnp.arange(slots, dtype=jnp.int32)
    live = (slot_ids[None, :] < counts[:, None]).astype(jnp.float32)
    rho = particles[:, 6]
    pressure = stiff * (rho - 1.0)
    volume = particles[:, 7] / rho * live
    ready = jnp.concatenate([particles[:, :6], pressure[:, None], volume[:, None]], axis=1)
    nearby = {0: ready}
    for offset in (1, -1, 2, -2):
        nearby[offset] = passed_along(ready, "flow", -offset)
    along = (jnp.arange(width) == 0).astype(jnp.float32)[:, None]
    stacked = jnp.stack([nearby[offset] + offset * along for offset in slab_order])
    stacked = lax.all_gather(stacked, "cross", axis=1, tiled=True)
    lookup = stacked.reshape((5 * slab_blk, width, slots))
    source_counts = jnp.max(jnp.where(lookup[:, 7] > 0.0, slot_ids[None, :] + 1, 0), axis=1)
    columns = jnp.swapaxes(ready, 1, 2)
    body = functools.partial(pair_kernel, per_block, 2.0 * GY, 2.0 * cells_z)
    return pl.pallas_call(
        body,
        out_shape=jax.ShapeDtypeStruct((blocks, 4, slots), jnp.float32),
        grid_spec=pltpu.PrefetchScalarGridSpec(
            num_scalar_prefetch=3,
            grid=(blocks,),
            in_specs=[
                pl.BlockSpec((1, width, slots), lambda i, *_: (i, 0, 0)),
                pl.BlockSpec((1, slots, width), lambda i, *_: (i, 0, 0)),
                pl.BlockSpec(memory_space=pltpu.VMEM),
            ],
            out_specs=pl.BlockSpec((1, 4, slots), lambda i, *_: (i, 0, 0)),
            scratch_shapes=[
                pltpu.VMEM((per_block + 2, 8, slots), jnp.float32),
                pltpu.VMEM((fields, slots, slots), jnp.float32),
                pltpu.VMEM((5, slots, slots), jnp.float32),
            ],
        ),
        compiler_params=pltpu.CompilerParams(vmem_limit_bytes=40 * 1024 * 1024),
        name="pair_rates",
    )(pairs.reshape(-1), counts, source_counts, particles, columns, lookup)


def solution(mesh):
    placed = (P(("flow", "cross"), None, None), P(("flow", "cross")), P(("flow", "cross"), None))
    return jax.shard_map(
        per_device,
        mesh=mesh,
        in_specs=placed,
        out_specs=P(("flow", "cross"), None, None),
        check_vma=False,
    )
```

```python
import functools
import math

import jax
import jax.numpy as jnp
from jax import lax
from jax.experimental import pallas as pl
from jax.experimental.pallas import tpu as pltpu
from jax.sharding import PartitionSpec as P

GY = 8


kernel_coef = 5.0 * 21.0 / (16.0 * math.pi)
eta_square = 0.01
sound_speed = 6.0
delta_coef = 0.1
visc_coef = 0.1
slab_order = (-2, -1, 0, 1, 2)
wave = sound_speed * visc_coef
stiff = sound_speed / visc_coef
rows_step = 16
tiles_step = 4
fields = 7


def passed_along(value, axis, steps):
    count = lax.axis_size(axis)
    pairs = [(source, (source + steps) % count) for source in range(count)]
    return lax.ppermute(value, axis, pairs)


def ready_kernel(counts, particles, out):
    blocks, width, slots = particles.shape
    lanes = lax.broadcasted_iota(jnp.int32, (1, slots), 1)

    def one(block, unused):
        rho = particles[block, 6:7, :]
        out[block, 0:6, :] = particles[block, 0:6, :]
        out[block, 6:7, :] = stiff * (rho - 1.0)
        out[block, 7:8, :] = jnp.where(lanes < counts[block], particles[block, 7:8, :] / rho, 0.0)
        return unused

    lax.fori_loop(0, blocks, one, 0, unroll=8)


def pair_kernel(per_block, slab_blk, wide_y, wide_z, codes, live_counts, source_counts, particles, ready, lookup, out, packed, spread, totals):
    blocks, width, slots = particles.shape
    lanes = lax.broadcasted_iota(jnp.int32, (8, slots), 1)
    row = lax.broadcasted_iota(jnp.int32, (8, slots), 0)
    wide = jnp.where(row == 1, wide_y, jnp.where(row == 2, wide_z, 0.0))
    inverse = jnp.where(row == 1, 1.0 / wide_y, jnp.where(row == 2, 1.0 / wide_z, 0.0))
    along = jnp.where(row == 0, 1.0, 0.0)
    empty = jnp.zeros((8, slots), jnp.float32)
    scale = kernel_coef / 8.0

    def finish(block):
        rows = []
        for which in range(5):
            total = empty
            for group in range(slots // 8):
                part = jnp.sum(totals[which, group * 8:group * 8 + 8, :], axis=1, keepdims=True)
                total = total + jnp.where(lanes == row + group * 8, part, 0.0)
            rows.append(jnp.sum(total, axis=0, keepdims=True))
        rho = particles[block, 6:7, :]
        drho = scale * (2.0 * delta_coef * sound_speed / stiff * rows[1] - rho * rows[0])
        over = (scale * wave) / rho
        alive = lanes[0:1] < live_counts[block]
        out[block, 0:1, :] = jnp.where(alive, drho, 0.0)
        for axis in range(3):
            out[block, axis + 1:axis + 2, :] = jnp.where(alive, over * rows[2 + axis], 0.0)

    def per_block_step(block, unused):
        finish(jnp.maximum(block - 1, 0))
        own = ready[block]
        own_first = jnp.broadcast_to(own[:, 0:1], (8, slots)) * inverse + 0.5

        current, tile, start = empty, jnp.int32(0), jnp.int32(0)
        for step in range(per_block):
            code = codes[block * per_block + step]
            count = source_counts[code]
            slab = jnp.int32(-2)
            for border in range(1, 5):
                slab = slab + (code >= border * slab_blk).astype(jnp.int32)
            value = lookup[code]
            first = jnp.broadcast_to(value[:, 0:1], (8, slots))
            value = value + (wide * jnp.floor(own_first - first * inverse) + along * slab.astype(jnp.float32))
            turned = pltpu.roll(value, start, 1)
            ahead = lanes >= start
            merged = jnp.where(ahead, turned, current)
            packed[tile] = merged
            end = start + count
            full = (end >= slots).astype(jnp.int32)
            keep = jnp.broadcast_to(full, (8, slots)) == 0
            rest = jnp.where(ahead, 0.0, turned)
            current = jnp.where(keep, merged, rest)
            tile = tile + full
            start = end - full * slots
        packed[tile] = current
        for more in range(1, tiles_step):
            packed[tile + more] = empty
        tiles = tile + (start > 0).astype(jnp.int32)

        columns = jnp.transpose(own)
        for group in range(slots // 8):
            for field in range(fields):
                spread[field, group * 8:group * 8 + 8, :] = jnp.broadcast_to(
                    columns[group * 8:group * 8 + 8, field:field + 1], (8, slots)
                )

        live = live_counts[block]

        def per_rows(index, unused):
            first = pl.multiple_of(index * rows_step, rows_step)
            rows = pl.ds(first, rows_step)
            xi, yi, zi, ui, vi, wi, pi = [spread[field, rows, :] for field in range(fields)]

            def one_tile(place, sums):
                s_close, s_diff, s_damp, s_x, s_y, s_z = sums
                xj, yj, zj, uj, vj, wj, pj, volume = [packed[place, field:field + 1, :] for field in range(8)]
                gap_x = xi - xj
                gap_y = yi - yj
                gap_z = zi - zj
                shifted = (gap_x * gap_x + eta_square) + (gap_y * gap_y + gap_z * gap_z)
                inv = lax.rsqrt(shifted)
                bump = jnp.maximum(2.0 - shifted * inv, 0.0)
                weight = (bump * bump) * (bump * volume)
                closing = (ui - uj) * gap_x + (vi - vj) * gap_y + (wi - wj) * gap_z
                inv_sq = inv * inv
                diff = weight * (pj - pi)
                push = weight * ((pi + pj) - closing * inv_sq)
                return (
                    s_close + weight * closing,
                    s_diff + diff,
                    s_damp + diff * inv_sq,
                    s_x + push * gap_x,
                    s_y + push * gap_y,
                    s_z + push * gap_z,
                )

            def some_tiles(place, sums):
                for more in range(tiles_step):
                    sums = one_tile(tiles_step * place + more, sums)
                return sums

            zero = jnp.zeros((rows_step, slots), jnp.float32)
            sums = lax.fori_loop(0, (tiles + tiles_step - 1) // tiles_step, some_tiles, (zero,) * 6)
            totals[0, rows, :] = sums[0]
            totals[1, rows, :] = sums[1] - eta_square * sums[2]
            totals[2, rows, :] = sums[3]
            totals[3, rows, :] = sums[4]
            totals[4, rows, :] = sums[5]
            return unused

        lax.fori_loop(0, (live + rows_step - 1) // rows_step, per_rows, 0)
        return unused

    lax.fori_loop(0, blocks, per_block_step, 0)
    finish(blocks - 1)


def per_device(particles, counts, pairs):
    blocks, width, slots = particles.shape
    slab_blk = blocks * lax.axis_size("cross")
    cells_z = slab_blk // GY
    per_block = pairs.shape[1]
    vmem = pl.BlockSpec(memory_space=pltpu.VMEM)
    smem = pl.BlockSpec(memory_space=pltpu.SMEM)
    limit = pltpu.CompilerParams(vmem_limit_bytes=40 * 1024 * 1024)
    ready = pl.pallas_call(
        ready_kernel,
        out_shape=jax.ShapeDtypeStruct(particles.shape, jnp.float32),
        in_specs=[smem, vmem],
        out_specs=vmem,
        compiler_params=limit,
        name="ready",
    )(counts, particles)
    nearby = {0: ready}
    for offset in (1, -1, 2, -2):
        nearby[offset] = passed_along(ready, "flow", -offset)
    stacked = jnp.stack([nearby[offset] for offset in slab_order])
    stacked = lax.all_gather(stacked, "cross", axis=1, tiled=True)
    lookup = stacked.reshape((5 * slab_blk, width, slots))
    slot_ids = jnp.arange(slots, dtype=jnp.int32)
    source_counts = jnp.max(jnp.where(lookup[:, 7] > 0.0, slot_ids[None, :] + 1, 0), axis=1)
    body = functools.partial(pair_kernel, per_block, slab_blk, 2.0 * GY, 2.0 * cells_z)
    return pl.pallas_call(
        body,
        out_shape=jax.ShapeDtypeStruct((blocks, 4, slots), jnp.float32),
        in_specs=[smem, smem, smem, vmem, vmem, vmem],
        out_specs=vmem,
        scratch_shapes=[
            pltpu.VMEM((per_block + tiles_step + 1, 8, slots), jnp.float32),
            pltpu.VMEM((fields, slots, slots), jnp.float32),
            pltpu.VMEM((5, slots, slots), jnp.float32),
        ],
        compiler_params=limit,
        name="pair_rates",
    )(pairs.reshape(-1), counts, source_counts, particles, ready, lookup)


def solution(mesh):
    placed = (P(("flow", "cross"), None, None), P(("flow", "cross")), P(("flow", "cross"), None))
    return jax.shard_map(
        per_device,
        mesh=mesh,
        in_specs=placed,
        out_specs=P(("flow", "cross"), None, None),
        check_vma=False,
    )
```

```python
import functools
import math

import jax
import jax.numpy as jnp
from jax import lax
from jax.experimental import pallas as pl
from jax.experimental.pallas import tpu as pltpu
from jax.sharding import PartitionSpec as P

GY = 8


kernel_coef = 5.0 * 21.0 / (16.0 * math.pi)
eta_square = 0.01
sound_speed = 6.0
delta_coef = 0.1
visc_coef = 0.1
slab_order = (-2, -1, 0, 1, 2)
wave = sound_speed * visc_coef
stiff = sound_speed / visc_coef
rows_step = 16
tiles_steps = (8, 4)
fields = 7


def passed_along(value, axis, steps):
    count = lax.axis_size(axis)
    pairs = [(source, (source + steps) % count) for source in range(count)]
    return lax.ppermute(value, axis, pairs)


def in_order(codes):
    places = jnp.arange(codes.shape[1], dtype=jnp.int32)
    mine, other = codes[:, :, None], codes[:, None, :]
    before = (other < mine) | ((other == mine) & (places[None, None, :] < places[None, :, None]))
    rank = jnp.sum(before.astype(jnp.int32), axis=2)
    return jnp.sum(jnp.where(rank[:, None, :] == places[None, :, None], codes[:, None, :], 0), axis=2)


def ready_kernel(counts, particles, out):
    blocks, width, slots = particles.shape
    lanes = lax.broadcasted_iota(jnp.int32, (1, slots), 1)

    def one(block, unused):
        rho = particles[block, 6:7, :]
        out[block, 0:6, :] = particles[block, 0:6, :]
        out[block, 6:7, :] = stiff * (rho - 1.0)
        out[block, 7:8, :] = jnp.where(lanes < counts[block], particles[block, 7:8, :] / rho, 0.0)
        return unused

    lax.fori_loop(0, blocks, one, 0, unroll=8)


def pair_kernel(slabs, wide_y, wide_z, codes, live_counts, source_counts, particles, ready, lookup, *rest_refs):
    earlier = rest_refs[0] if len(rest_refs) == 5 else None
    out, packed, spread, totals = rest_refs[-4:]
    per_block = len(slabs)
    blocks, width, slots = particles.shape
    lanes = lax.broadcasted_iota(jnp.int32, (8, slots), 1)
    row = lax.broadcasted_iota(jnp.int32, (8, slots), 0)
    wide = jnp.where(row == 1, wide_y, jnp.where(row == 2, wide_z, 0.0))
    inverse = jnp.where(row == 1, 1.0 / wide_y, jnp.where(row == 2, 1.0 / wide_z, 0.0))
    along = jnp.where(row == 0, 1.0, 0.0)
    empty = jnp.zeros((8, slots), jnp.float32)
    scale = kernel_coef / 8.0

    def finish(block):
        rows = []
        for which in range(5):
            total = empty
            for group in range(slots // 8):
                part = jnp.sum(totals[which, group * 8:group * 8 + 8, :], axis=1, keepdims=True)
                total = total + jnp.where(lanes == row + group * 8, part, 0.0)
            rows.append(jnp.sum(total, axis=0, keepdims=True))
        rho = particles[block, 6:7, :]
        drho = scale * (2.0 * delta_coef * sound_speed / stiff * rows[1] - rho * rows[0])
        over = (scale * wave) / rho
        alive = lanes[0:1] < live_counts[block]
        results = [drho] + [over * rows[2 + axis] for axis in range(3)]
        for place, result in enumerate(results):
            if earlier is not None:
                result = result + earlier[block, place:place + 1, :]
            out[block, place:place + 1, :] = jnp.where(alive, result, 0.0)

    def per_block_step(block, unused):
        finish(jnp.maximum(block - 1, 0))
        own = ready[block]
        own_first = jnp.broadcast_to(own[:, 0:1], (8, slots)) * inverse + 0.5

        current, tile, start = empty, jnp.int32(0), jnp.int32(0)
        for step in range(per_block):
            code = codes[block * per_block + step]
            count = source_counts[code]
            value = lookup[code]
            first = jnp.broadcast_to(value[:, 0:1], (8, slots))
            value = value + (wide * jnp.floor(own_first - first * inverse) + along * slabs[step])
            turned = pltpu.roll(value, start, 1)
            ahead = lanes >= start
            merged = jnp.where(ahead, turned, current)
            packed[tile] = merged
            end = start + count
            full = (end >= slots).astype(jnp.int32)
            keep = jnp.broadcast_to(full, (8, slots)) == 0
            rest = jnp.where(ahead, 0.0, turned)
            current = jnp.where(keep, merged, rest)
            tile = tile + full
            start = end - full * slots
        packed[tile] = current
        for more in range(1, tiles_steps[-1]):
            packed[tile + more] = empty
        tiles = tile + (start > 0).astype(jnp.int32)

        columns = jnp.transpose(own)
        for group in range(slots // 8):
            for field in range(fields):
                spread[field, group * 8:group * 8 + 8, :] = jnp.broadcast_to(
                    columns[group * 8:group * 8 + 8, field:field + 1], (8, slots)
                )

        live = live_counts[block]

        def per_rows(index, unused):
            first = pl.multiple_of(index * rows_step, rows_step)
            rows = pl.ds(first, rows_step)
            xi, yi, zi, ui, vi, wi, pi = [spread[field, rows, :] for field in range(fields)]

            def one_tile(place, sums):
                s_close, s_diff, s_damp, s_x, s_y, s_z = sums
                xj, yj, zj, uj, vj, wj, pj, volume = [packed[place, field:field + 1, :] for field in range(8)]
                gap_x = xi - xj
                gap_y = yi - yj
                gap_z = zi - zj
                shifted = (gap_x * gap_x + eta_square) + (gap_y * gap_y + gap_z * gap_z)
                inv = lax.rsqrt(shifted)
                bump = jnp.maximum(2.0 - shifted * inv, 0.0)
                weight = (bump * bump) * (bump * volume)
                closing = (ui - uj) * gap_x + (vi - vj) * gap_y + (wi - wj) * gap_z
                inv_sq = inv * inv
                diff = weight * (pj - pi)
                push = weight * ((pi + pj) - closing * inv_sq)
                return (
                    s_close + weight * closing,
                    s_diff + diff,
                    s_damp + diff * inv_sq,
                    s_x + push * gap_x,
                    s_y + push * gap_y,
                    s_z + push * gap_z,
                )

            sums = (jnp.zeros((rows_step, slots), jnp.float32),) * 6
            begin = jnp.int32(0)
            for step in tiles_steps:
                last = step == tiles_steps[-1]
                turns = (tiles - begin + (step - 1 if last else 0)) // step

                def some_tiles(turn, sums, step=step, begin=begin):
                    for more in range(step):
                        sums = one_tile(begin + turn * step + more, sums)
                    return sums

                sums = lax.fori_loop(0, turns, some_tiles, sums)
                begin = begin + turns * step
            totals[0, rows, :] = sums[0]
            totals[1, rows, :] = sums[1] - eta_square * sums[2]
            totals[2, rows, :] = sums[3]
            totals[3, rows, :] = sums[4]
            totals[4, rows, :] = sums[5]
            return unused

        lax.fori_loop(0, (live + rows_step - 1) // rows_step, per_rows, 0)
        return unused

    lax.fori_loop(0, blocks, per_block_step, 0)
    finish(blocks - 1)


def per_device(particles, counts, pairs):
    blocks, width, slots = particles.shape
    slab_blk = blocks * lax.axis_size("cross")
    cells_z = slab_blk // GY
    per_block = pairs.shape[1]
    vmem = pl.BlockSpec(memory_space=pltpu.VMEM)
    smem = pl.BlockSpec(memory_space=pltpu.SMEM)
    limit = pltpu.CompilerParams(vmem_limit_bytes=40 * 1024 * 1024)
    ready = pl.pallas_call(
        ready_kernel,
        out_shape=jax.ShapeDtypeStruct(particles.shape, jnp.float32),
        in_specs=[smem, vmem],
        out_specs=vmem,
        compiler_params=limit,
        name="ready",
    )(counts, particles)
    nearby = {offset: passed_along(ready, "flow", -offset) for offset in slab_order if offset}
    listed = in_order(pairs)
    per_slab = per_block // len(slab_order)
    middle = per_slab * (len(slab_order) // 2)
    own_codes = listed[:, middle:middle + per_slab] - 2 * slab_blk
    far_codes = jnp.concatenate([listed[:, :middle], listed[:, middle + per_slab:] - slab_blk], axis=1)
    own_lookup = lax.all_gather(ready, "cross", axis=0, tiled=True)
    stacked = jnp.stack([nearby[offset] for offset in slab_order if offset])
    stacked, own_lookup = lax.optimization_barrier((stacked, own_lookup))
    far_lookup = lax.all_gather(stacked, "cross", axis=1, tiled=True)
    far_lookup = far_lookup.reshape((4 * slab_blk, width, slots))

    def rates(slabs, codes, lookup, earlier, name):
        slot_ids = jnp.arange(slots, dtype=jnp.int32)
        source_counts = jnp.max(jnp.where(lookup[:, 7] > 0.0, slot_ids[None, :] + 1, 0), axis=1)
        work = blocks * slots * slots * len(slabs)
        return pl.pallas_call(
            functools.partial(pair_kernel, slabs, 2.0 * GY, 2.0 * cells_z),
            out_shape=jax.ShapeDtypeStruct((blocks, 4, slots), jnp.float32),
            in_specs=[smem, smem, smem, vmem, vmem, vmem] + [vmem] * len(earlier),
            out_specs=vmem,
            scratch_shapes=[
                pltpu.VMEM((len(slabs) + max(tiles_steps) + 1, 8, slots), jnp.float32),
                pltpu.VMEM((fields, slots, slots), jnp.float32),
                pltpu.VMEM((5, slots, slots), jnp.float32),
            ],
            compiler_params=limit,
            cost_estimate=pl.CostEstimate(flops=60 * work, bytes_accessed=4 * lookup.size, transcendentals=work),
            name=name,
        )(codes.reshape(-1), counts, source_counts, particles, ready, lookup, *earlier)

    own_rates = rates((0.0,) * per_slab, own_codes, own_lookup, (), "own_slab")
    far_slabs = tuple(float(offset) for offset in slab_order if offset for _ in range(per_slab))
    return rates(far_slabs, far_codes, far_lookup, (own_rates,), "other_slabs")


def solution(mesh):
    placed = (P(("flow", "cross"), None, None), P(("flow", "cross")), P(("flow", "cross"), None))
    return jax.shard_map(
        per_device,
        mesh=mesh,
        in_specs=placed,
        out_specs=P(("flow", "cross"), None, None),
        check_vma=False,
    )
```

```python
import functools
import math

import jax
import jax.numpy as jnp
from jax import lax
from jax.experimental import pallas as pl
from jax.experimental.pallas import tpu as pltpu
from jax.sharding import PartitionSpec as P

GY = 8


kernel_coef = 5.0 * 21.0 / (16.0 * math.pi)
eta_square = 0.01
sound_speed = 6.0
delta_coef = 0.1
visc_coef = 0.1
slab_order = (-2, -1, 0, 1, 2)
wave = sound_speed * visc_coef
stiff = sound_speed / visc_coef
rows_step = 16
tiles_steps = (8, 4)
fields = 7


def passed_along(value, axis, steps):
    count = lax.axis_size(axis)
    pairs = [(source, (source + steps) % count) for source in range(count)]
    return lax.ppermute(value, axis, pairs)


def in_order(codes):
    places = jnp.arange(codes.shape[1], dtype=jnp.int32)
    mine, other = codes[:, :, None], codes[:, None, :]
    before = (other < mine) | ((other == mine) & (places[None, None, :] < places[None, :, None]))
    rank = jnp.sum(before.astype(jnp.int32), axis=2)
    return jnp.sum(jnp.where(rank[:, None, :] == places[None, :, None], codes[:, None, :], 0), axis=2)


def ready_kernel(counts, particles, out):
    blocks, width, slots = particles.shape
    lanes = lax.broadcasted_iota(jnp.int32, (1, slots), 1)

    def one(block, unused):
        rho = particles[block, 6:7, :]
        out[block, 0:6, :] = particles[block, 0:6, :]
        out[block, 6:7, :] = stiff * (rho - 1.0)
        out[block, 7:8, :] = jnp.where(lanes < counts[block], particles[block, 7:8, :] / rho, 0.0)
        return unused

    lax.fori_loop(0, blocks, one, 0, unroll=8)


def pair_kernel(slabs, per_slab, wide_y, wide_z, codes, live_counts, source_counts, ready, lookup, spread, *rest_refs):
    last_call = len(rest_refs) == 5
    block = pl.program_id(0)
    blocks, width, slots = ready.shape
    lanes = lax.broadcasted_iota(jnp.int32, (8, slots), 1)
    row = lax.broadcasted_iota(jnp.int32, (8, slots), 0)
    wide = jnp.where(row == 1, wide_y, jnp.where(row == 2, wide_z, 0.0))
    inverse = jnp.where(row == 1, 1.0 / wide_y, jnp.where(row == 2, 1.0 / wide_z, 0.0))
    along = jnp.where(row == 0, 1.0, 0.0)
    empty = jnp.zeros((8, slots), jnp.float32)
    scale = kernel_coef / 8.0
    if last_call:
        particles, earlier, out, packed, totals = rest_refs
    else:
        totals, packed = rest_refs
        totals = totals.at[0]

    def finish(block):
        rows = []
        for which in range(5):
            total = empty
            for group in range(slots // 8):
                part = jnp.sum(totals[which, group * 8:group * 8 + 8, :], axis=1, keepdims=True)
                total = total + jnp.where(lanes == row + group * 8, part, 0.0)
            rows.append(jnp.sum(total, axis=0, keepdims=True))
        rho = particles[block, 6:7, :]
        drho = scale * (2.0 * delta_coef * sound_speed / stiff * rows[1] - rho * rows[0])
        over = (scale * wave) / rho
        alive = lanes[0:1] < live_counts[block]
        out[block, 0:1, :] = jnp.where(alive, drho, 0.0)
        for axis in range(3):
            out[block, axis + 1:axis + 2, :] = jnp.where(alive, over * rows[2 + axis], 0.0)

    if last_call:
        finish(jnp.maximum(block - 1, 0))
    own = ready[block]
    own_first = jnp.broadcast_to(own[:, 0:1], (8, slots)) * inverse + 0.5

    current, tile, start = empty, jnp.int32(0), jnp.int32(0)
    shifts = []
    for step in range(len(slabs) * per_slab):
        slab, cell = divmod(step, per_slab)
        code = codes[block * (len(slabs) * per_slab) + step]
        count = source_counts[code]
        value = lookup[code]
        if slab == 0:
            first = jnp.broadcast_to(value[:, 0:1], (8, slots))
            shifts.append(wide * jnp.floor(own_first - first * inverse))
        value = value + (shifts[cell] + along * slabs[slab])
        turned = pltpu.roll(value, start, 1)
        ahead = lanes >= start
        merged = jnp.where(ahead, turned, current)
        packed[tile] = merged
        end = start + count
        full = (end >= slots).astype(jnp.int32)
        keep = jnp.broadcast_to(full, (8, slots)) == 0
        rest = jnp.where(ahead, 0.0, turned)
        current = jnp.where(keep, merged, rest)
        tile = tile + full
        start = end - full * slots
    packed[tile] = current
    for more in range(1, tiles_steps[-1]):
        packed[tile + more] = empty
    tiles = tile + (start > 0).astype(jnp.int32)
    live = live_counts[block]

    def per_rows(index, unused):
        first = pl.multiple_of(index * rows_step, rows_step)
        rows = pl.ds(first, rows_step)
        xi, yi, zi, ui, vi, wi, pi = [spread[0, field, rows, :] for field in range(fields)]

        def one_tile(place, sums):
            s_close, s_diff, s_damp, s_x, s_y, s_z = sums
            xj, yj, zj, uj, vj, wj, pj, volume = [packed[place, field:field + 1, :] for field in range(8)]
            gap_x = xi - xj
            gap_y = yi - yj
            gap_z = zi - zj
            shifted = (gap_x * gap_x + eta_square) + (gap_y * gap_y + gap_z * gap_z)
            inv = lax.rsqrt(shifted)
            bump = jnp.maximum(2.0 - shifted * inv, 0.0)
            weight = (bump * bump) * (bump * volume)
            closing = (ui - uj) * gap_x + (vi - vj) * gap_y + (wi - wj) * gap_z
            inv_sq = inv * inv
            diff = weight * (pj - pi)
            push = weight * ((pi + pj) - closing * inv_sq)
            return (
                s_close + weight * closing,
                s_diff + diff,
                s_damp + diff * inv_sq,
                s_x + push * gap_x,
                s_y + push * gap_y,
                s_z + push * gap_z,
            )

        zero = jnp.zeros((rows_step, slots), jnp.float32)
        if last_call:
            sums = [earlier[0, which, rows, :] for which in range(5)]
            sums = (sums[0], sums[1], zero, sums[2], sums[3], sums[4])
        else:
            sums = (zero,) * 6
        begin = jnp.int32(0)
        for step in tiles_steps:
            last = step == tiles_steps[-1]
            turns = (tiles - begin + (step - 1 if last else 0)) // step

            def some_tiles(turn, sums, step=step, begin=begin):
                for more in range(step):
                    sums = one_tile(begin + turn * step + more, sums)
                return sums

            sums = lax.fori_loop(0, turns, some_tiles, sums)
            begin = begin + turns * step
        totals[0, rows, :] = sums[0]
        totals[1, rows, :] = sums[1] - eta_square * sums[2]
        totals[2, rows, :] = sums[3]
        totals[3, rows, :] = sums[4]
        totals[4, rows, :] = sums[5]
        return unused

    lax.fori_loop(0, (live + rows_step - 1) // rows_step, per_rows, 0)

    if last_call:
        @pl.when(block == blocks - 1)
        def _():
            finish(block)


def per_device(particles, counts, pairs):
    blocks, width, slots = particles.shape
    slab_blk = blocks * lax.axis_size("cross")
    cells_z = slab_blk // GY
    per_block = pairs.shape[1]
    vmem = pl.BlockSpec(memory_space=pltpu.VMEM)
    smem = pl.BlockSpec(memory_space=pltpu.SMEM)
    limit = pltpu.CompilerParams(vmem_limit_bytes=40 * 1024 * 1024)
    ready = pl.pallas_call(
        ready_kernel,
        out_shape=jax.ShapeDtypeStruct(particles.shape, jnp.float32),
        in_specs=[smem, vmem],
        out_specs=vmem,
        compiler_params=limit,
        name="ready",
    )(counts, particles)
    nearby = {offset: passed_along(ready, "flow", -offset) for offset in slab_order if offset}
    listed = in_order(pairs)
    per_slab = per_block // len(slab_order)
    middle = per_slab * (len(slab_order) // 2)
    own_codes = listed[:, middle:middle + per_slab] - 2 * slab_blk
    far_codes = jnp.concatenate([listed[:, :middle], listed[:, middle + per_slab:] - slab_blk], axis=1)
    own_lookup = lax.all_gather(ready, "cross", axis=0, tiled=True)
    stacked = jnp.stack([nearby[offset] for offset in slab_order if offset])
    spread = jnp.broadcast_to(ready[:, :fields, :, None], (blocks, fields, slots, slots))
    stacked, own_lookup, spread = lax.optimization_barrier((stacked, own_lookup, spread))
    far_lookup = lax.all_gather(stacked, "cross", axis=1, tiled=True)
    far_lookup = far_lookup.reshape((4 * slab_blk, width, slots))


    def sums(slabs, codes, lookup, more, name):
        slot_ids = jnp.arange(slots, dtype=jnp.int32)
        source_counts = jnp.max(jnp.where(lookup[:, 7] > 0.0, slot_ids[None, :] + 1, 0), axis=1)
        work = blocks * slots * slots * len(slabs) * per_slab
        rates = jax.ShapeDtypeStruct((blocks, 4, slots), jnp.float32)
        totals = jax.ShapeDtypeStruct((blocks, 5, slots, slots), jnp.float32)
        by_block = pl.BlockSpec((1, 5, slots, slots), lambda i: (i, 0, 0, 0))
        scratch = [pltpu.VMEM((len(slabs) * per_slab + max(tiles_steps) + 1, 8, slots), jnp.float32)]
        if more:
            scratch.append(pltpu.VMEM((5, slots, slots), jnp.float32))
        return pl.pallas_call(
            functools.partial(pair_kernel, slabs, per_slab, 2.0 * GY, 2.0 * cells_z),
            out_shape=rates if more else totals,
            grid=(blocks,),
            in_specs=[smem, smem, smem, vmem, vmem]
            + [pl.BlockSpec((1, fields, slots, slots), lambda i: (i, 0, 0, 0))]
            + ([vmem, by_block] if more else []),
            out_specs=vmem if more else by_block,
            scratch_shapes=scratch,
            compiler_params=limit,
            cost_estimate=pl.CostEstimate(flops=60 * work, bytes_accessed=4 * lookup.size, transcendentals=work),
            name=name,
        )(codes.reshape(-1), counts, source_counts, ready, lookup, spread, *more)

    own_sums = sums((0.0,), own_codes, own_lookup, (), "own_slab")
    far_slabs = tuple(float(offset) for offset in slab_order if offset)
    return sums(far_slabs, far_codes, far_lookup, (particles, own_sums), "other_slabs")


def solution(mesh):
    placed = (P(("flow", "cross"), None, None), P(("flow", "cross")), P(("flow", "cross"), None))
    return jax.shard_map(
        per_device,
        mesh=mesh,
        in_specs=placed,
        out_specs=P(("flow", "cross"), None, None),
        check_vma=False,
    )
```

```python
import functools
import math

import jax
import jax.numpy as jnp
from jax import lax
from jax.experimental import pallas as pl
from jax.experimental.pallas import tpu as pltpu
from jax.sharding import PartitionSpec as P

GY = 8


kernel_coef = 5.0 * 21.0 / (16.0 * math.pi)
eta_square = 0.01
sound_speed = 6.0
delta_coef = 0.1
visc_coef = 0.1
slab_order = (-2, -1, 0, 1, 2)
wave = sound_speed * visc_coef
stiff = sound_speed / visc_coef
rows_step = 16
tail_step = 4
fields = 7


def passed_along(value, axis, steps):
    count = lax.axis_size(axis)
    pairs = [(source, (source + steps) % count) for source in range(count)]
    return lax.ppermute(value, axis, pairs)


def in_order(codes):
    places = jnp.arange(codes.shape[1], dtype=jnp.int32)
    mine, other = codes[:, :, None], codes[:, None, :]
    before = (other < mine) | ((other == mine) & (places[None, None, :] < places[None, :, None]))
    rank = jnp.sum(before.astype(jnp.int32), axis=2)
    return jnp.sum(jnp.where(rank[:, None, :] == places[None, :, None], codes[:, None, :], 0), axis=2)


def ready_kernel(counts, particles, out):
    blocks, width, slots = particles.shape
    lanes = lax.broadcasted_iota(jnp.int32, (1, slots), 1)

    def one(block, unused):
        rho = particles[block, 6:7, :]
        out[block, 0:6, :] = particles[block, 0:6, :]
        out[block, 6:7, :] = stiff * (rho - 1.0)
        out[block, 7:8, :] = jnp.where(lanes < counts[block], particles[block, 7:8, :] / rho, 0.0)
        return unused

    lax.fori_loop(0, blocks, one, 0, unroll=8)


def pair_kernel(main_step, slabs, per_slab, wide_y, wide_z, codes, live_counts, source_counts, ready, lookup, spread, *rest_refs):
    last_call = len(rest_refs) == 5
    block = pl.program_id(0)
    blocks, width, slots = ready.shape
    lanes = lax.broadcasted_iota(jnp.int32, (8, slots), 1)
    row = lax.broadcasted_iota(jnp.int32, (8, slots), 0)
    wide = jnp.where(row == 1, wide_y, jnp.where(row == 2, wide_z, 0.0))
    inverse = jnp.where(row == 1, 1.0 / wide_y, jnp.where(row == 2, 1.0 / wide_z, 0.0))
    along = jnp.where(row == 0, 1.0, 0.0)
    empty = jnp.zeros((8, slots), jnp.float32)
    scale = kernel_coef / 8.0
    if last_call:
        particles, earlier, out, packed, totals = rest_refs
    else:
        totals, packed = rest_refs
        totals = totals.at[0]

    def finish(block):
        rows = []
        for which in range(5):
            total = empty
            for group in range(slots // 8):
                part = jnp.sum(totals[which, group * 8:group * 8 + 8, :], axis=1, keepdims=True)
                total = total + jnp.where(lanes == row + group * 8, part, 0.0)
            rows.append(jnp.sum(total, axis=0, keepdims=True))
        rho = particles[block, 6:7, :]
        drho = scale * (2.0 * delta_coef * sound_speed / stiff * rows[1] - rho * rows[0])
        over = (scale * wave) / rho
        alive = lanes[0:1] < live_counts[block]
        out[block, 0:1, :] = jnp.where(alive, drho, 0.0)
        for axis in range(3):
            out[block, axis + 1:axis + 2, :] = jnp.where(alive, over * rows[2 + axis], 0.0)

    if last_call:
        finish(jnp.maximum(block - 1, 0))
    own = ready[block]
    own_first = jnp.broadcast_to(own[:, 0:1], (8, slots)) * inverse + 0.5

    current, tile, start = empty, jnp.int32(0), jnp.int32(0)
    shifts = []
    for step in range(len(slabs) * per_slab):
        slab, cell = divmod(step, per_slab)
        code = codes[block * (len(slabs) * per_slab) + step]
        count = source_counts[code]
        value = lookup[code]
        if slab == 0:
            first = jnp.broadcast_to(value[:, 0:1], (8, slots))
            shifts.append(wide * jnp.floor(own_first - first * inverse))
        value = value + (shifts[cell] + along * slabs[slab])
        turned = pltpu.roll(value, start, 1)
        ahead = lanes >= start
        merged = jnp.where(ahead, turned, current)
        packed[tile] = merged
        end = start + count
        full = (end >= slots).astype(jnp.int32)
        keep = jnp.broadcast_to(full, (8, slots)) == 0
        rest = jnp.where(ahead, 0.0, turned)
        current = jnp.where(keep, merged, rest)
        tile = tile + full
        start = end - full * slots
    packed[tile] = current
    for more in range(1, tail_step):
        packed[tile + more] = empty
    tiles = tile + (start > 0).astype(jnp.int32)
    live = live_counts[block]

    def per_rows(index, unused):
        first = pl.multiple_of(index * rows_step, rows_step)
        rows = pl.ds(first, rows_step)
        xi, yi, zi, ui, vi, wi, pi = [spread[0, field, rows, :] for field in range(fields)]

        def one_tile(place, sums):
            s_close, s_diff, s_damp, s_x, s_y, s_z = sums
            xj, yj, zj, uj, vj, wj, pj, volume = [packed[place, field:field + 1, :] for field in range(8)]
            gap_x = xi - xj
            gap_y = yi - yj
            gap_z = zi - zj
            shifted = (gap_x * gap_x + eta_square) + (gap_y * gap_y + gap_z * gap_z)
            inv = lax.rsqrt(shifted)
            bump = jnp.maximum(2.0 - shifted * inv, 0.0)
            weight = (bump * bump) * (bump * volume)
            closing = (ui - uj) * gap_x + (vi - vj) * gap_y + (wi - wj) * gap_z
            inv_sq = inv * inv
            diff = weight * (pj - pi)
            push = weight * ((pi + pj) - closing * inv_sq)
            return (
                s_close + weight * closing,
                s_diff + diff,
                s_damp + diff * inv_sq,
                s_x + push * gap_x,
                s_y + push * gap_y,
                s_z + push * gap_z,
            )

        zero = jnp.zeros((rows_step, slots), jnp.float32)
        if last_call:
            sums = [earlier[0, which, rows, :] for which in range(5)]
            sums = (sums[0], sums[1], zero, sums[2], sums[3], sums[4])
        else:
            sums = (zero,) * 6
        def some_tiles(step, begin):
            def body(turn, sums):
                for more in range(step):
                    sums = one_tile(begin + turn * step + more, sums)
                return sums
            return body

        turns = (tiles + tail_step - 1) // main_step
        begin = turns * main_step
        tails = (jnp.maximum(tiles - begin, 0) + tail_step - 1) // tail_step
        sums = lax.fori_loop(0, turns, some_tiles(main_step, 0), sums)
        sums = lax.fori_loop(0, tails, some_tiles(tail_step, begin), sums)
        totals[0, rows, :] = sums[0]
        totals[1, rows, :] = sums[1] - eta_square * sums[2]
        totals[2, rows, :] = sums[3]
        totals[3, rows, :] = sums[4]
        totals[4, rows, :] = sums[5]
        return unused

    lax.fori_loop(0, (live + rows_step - 1) // rows_step, per_rows, 0)

    if last_call:
        @pl.when(block == blocks - 1)
        def _():
            finish(block)


def per_device(particles, counts, pairs):
    blocks, width, slots = particles.shape
    slab_blk = blocks * lax.axis_size("cross")
    cells_z = slab_blk // GY
    per_block = pairs.shape[1]
    vmem = pl.BlockSpec(memory_space=pltpu.VMEM)
    smem = pl.BlockSpec(memory_space=pltpu.SMEM)
    limit = pltpu.CompilerParams(vmem_limit_bytes=40 * 1024 * 1024)
    ready = pl.pallas_call(
        ready_kernel,
        out_shape=jax.ShapeDtypeStruct(particles.shape, jnp.float32),
        in_specs=[smem, vmem],
        out_specs=vmem,
        compiler_params=limit,
        name="ready",
    )(counts, particles)
    nearby = {offset: passed_along(ready, "flow", -offset) for offset in (-2, 2, -1)}
    spread = jnp.broadcast_to(ready[:, :fields, :, None], (blocks, fields, slots, slots))
    spread, held = lax.optimization_barrier((spread, ready))
    nearby[1] = passed_along(held, "flow", -1)
    listed = in_order(pairs)
    per_slab = per_block // len(slab_order)
    middle = per_slab * (len(slab_order) // 2)
    own_codes = listed[:, middle:middle + per_slab] - 2 * slab_blk
    far_codes = jnp.concatenate([listed[:, :middle], listed[:, middle + per_slab:] - slab_blk], axis=1)
    own_lookup = lax.all_gather(ready, "cross", axis=0, tiled=True)
    stacked = jnp.stack([nearby[offset] for offset in slab_order if offset])
    stacked, own_lookup = lax.optimization_barrier((stacked, own_lookup))
    far_lookup = lax.all_gather(stacked, "cross", axis=1, tiled=True)
    far_lookup = far_lookup.reshape((4 * slab_blk, width, slots))


    def sums(main_step, slabs, codes, lookup, more, name):
        slot_ids = jnp.arange(slots, dtype=jnp.int32)
        source_counts = jnp.max(jnp.where(lookup[:, 7] > 0.0, slot_ids[None, :] + 1, 0), axis=1)
        work = blocks * slots * slots * len(slabs) * per_slab
        rates = jax.ShapeDtypeStruct((blocks, 4, slots), jnp.float32)
        totals = jax.ShapeDtypeStruct((blocks, 5, slots, slots), jnp.float32)
        by_block = pl.BlockSpec((1, 5, slots, slots), lambda i: (i, 0, 0, 0))
        scratch = [pltpu.VMEM((len(slabs) * per_slab + main_step + tail_step, 8, slots), jnp.float32)]
        if more:
            scratch.append(pltpu.VMEM((5, slots, slots), jnp.float32))
        return pl.pallas_call(
            functools.partial(pair_kernel, main_step, slabs, per_slab, 2.0 * GY, 2.0 * cells_z),
            out_shape=rates if more else totals,
            grid=(blocks,),
            in_specs=[smem, smem, smem, vmem, vmem]
            + [pl.BlockSpec((1, fields, slots, slots), lambda i: (i, 0, 0, 0))]
            + ([vmem, by_block] if more else []),
            out_specs=vmem if more else by_block,
            scratch_shapes=scratch,
            compiler_params=limit,
            cost_estimate=pl.CostEstimate(flops=60 * work, bytes_accessed=4 * lookup.size, transcendentals=work),
            name=name,
        )(codes.reshape(-1), counts, source_counts, ready, lookup, spread, *more)

    own_sums = sums(8, (0.0,), own_codes, own_lookup, (), "own_slab")
    far_slabs = tuple(float(offset) for offset in slab_order if offset)
    return sums(12, far_slabs, far_codes, far_lookup, (particles, own_sums), "other_slabs")


def solution(mesh):
    placed = (P(("flow", "cross"), None, None), P(("flow", "cross")), P(("flow", "cross"), None))
    return jax.shard_map(
        per_device,
        mesh=mesh,
        in_specs=placed,
        out_specs=P(("flow", "cross"), None, None),
        check_vma=False,
    )
```

```python
import functools
import math

import jax
import jax.numpy as jnp
from jax import lax
from jax.experimental import pallas as pl
from jax.experimental.pallas import tpu as pltpu
from jax.sharding import PartitionSpec as P

GY = 8


kernel_coef = 5.0 * 21.0 / (16.0 * math.pi)
eta_square = 0.01
sound_speed = 6.0
delta_coef = 0.1
visc_coef = 0.1
slab_order = (-2, -1, 0, 1, 2)
wave = sound_speed * visc_coef
stiff = sound_speed / visc_coef
rows_step = 16
tail_step = 4
fields = 7


def passed_along(value, axis, steps):
    count = lax.axis_size(axis)
    pairs = [(source, (source + steps) % count) for source in range(count)]
    return lax.ppermute(value, axis, pairs)


def in_order(codes):
    places = jnp.arange(codes.shape[1], dtype=jnp.int32)
    mine, other = codes[:, :, None], codes[:, None, :]
    before = (other < mine) | ((other == mine) & (places[None, None, :] < places[None, :, None]))
    rank = jnp.sum(before.astype(jnp.int32), axis=2)
    return jnp.sum(jnp.where(rank[:, None, :] == places[None, :, None], codes[:, None, :], 0), axis=2)


def ready_kernel(counts, particles, out):
    blocks, width, slots = particles.shape
    lanes = lax.broadcasted_iota(jnp.int32, (1, slots), 1)

    def one(block, unused):
        rho = particles[block, 6:7, :]
        out[block, 0:6, :] = particles[block, 0:6, :]
        out[block, 6:7, :] = stiff * (rho - 1.0)
        out[block, 7:8, :] = jnp.where(lanes < counts[block], particles[block, 7:8, :] / rho, 0.0)
        return unused

    lax.fori_loop(0, blocks, one, 0, unroll=8)


def pair_kernel(main_step, slabs, per_slab, wide_y, wide_z, codes, live_counts, source_counts, ready, lookup, *rest_refs):
    spread, rest_refs = rest_refs[:fields], rest_refs[fields:]
    earlier = rest_refs[0] if len(rest_refs) == 5 else None
    particles, out, packed, totals = rest_refs[-4:]
    block = pl.program_id(0)
    blocks, width, slots = ready.shape
    lanes = lax.broadcasted_iota(jnp.int32, (8, slots), 1)
    row = lax.broadcasted_iota(jnp.int32, (8, slots), 0)
    wide = jnp.where(row == 1, wide_y, jnp.where(row == 2, wide_z, 0.0))
    inverse = jnp.where(row == 1, 1.0 / wide_y, jnp.where(row == 2, 1.0 / wide_z, 0.0))
    along = jnp.where(row == 0, 1.0, 0.0)
    empty = jnp.zeros((8, slots), jnp.float32)
    scale = kernel_coef / 8.0
    def finish(block):
        every = totals[...]
        high = every.astype(jnp.bfloat16)
        low = (every - high.astype(jnp.float32)).astype(jnp.bfloat16)
        ones = jnp.ones((2 * slots, slots), jnp.bfloat16)
        every = jnp.dot(jnp.concatenate([high, low], axis=1), ones, preferred_element_type=jnp.float32)
        rows = []
        for which in range(5):
            total = empty
            for group in range(slots // 8):
                begin = which * slots + group * 8
                total = total + jnp.where(lanes == row + group * 8, every[begin:begin + 8], 0.0)
            rows.append(jnp.sum(total, axis=0, keepdims=True))
        rho = particles[block, 6:7, :]
        drho = scale * (2.0 * delta_coef * sound_speed / stiff * rows[1] - rho * rows[0])
        over = (scale * wave) / rho
        alive = lanes[0:1] < live_counts[block]
        results = [drho] + [over * rows[2 + axis] for axis in range(3)]
        for place, result in enumerate(results):
            if earlier is not None:
                result = result + earlier[block, place:place + 1, :]
            out[block, place:place + 1, :] = jnp.where(alive, result, 0.0)

    finish(jnp.maximum(block - 1, 0))
    own = ready[block]
    own_first = jnp.broadcast_to(own[:, 0:1], (8, slots)) * inverse + 0.5

    current, tile, start = empty, jnp.int32(0), jnp.int32(0)
    shifts = []
    for step in range(len(slabs) * per_slab):
        slab, cell = divmod(step, per_slab)
        code = codes[block * (len(slabs) * per_slab) + step]
        count = source_counts[code]
        value = lookup[code]
        if slab == 0:
            first = jnp.broadcast_to(value[:, 0:1], (8, slots))
            shifts.append(wide * jnp.floor(own_first - first * inverse))
        value = value + (shifts[cell] + along * slabs[slab])
        turned = pltpu.roll(value, start, 1)
        ahead = lanes >= start
        merged = jnp.where(ahead, turned, current)
        packed[tile] = merged
        end = start + count
        full = (end >= slots).astype(jnp.int32)
        keep = jnp.broadcast_to(full, (8, slots)) == 0
        rest = jnp.where(ahead, 0.0, turned)
        current = jnp.where(keep, merged, rest)
        tile = tile + full
        start = end - full * slots
    packed[tile] = current
    for more in range(1, tail_step):
        packed[tile + more] = empty
    tiles = tile + (start > 0).astype(jnp.int32)
    live = live_counts[block]

    def per_rows(index, unused):
        first = pl.multiple_of(index * rows_step, rows_step)
        rows = pl.ds(first, rows_step)
        xi, yi, zi, ui, vi, wi, pi = [spread[field][0, 0, rows, :] for field in range(fields)]

        def one_tile(place, sums):
            s_close, s_diff, s_damp, s_x, s_y, s_z = sums
            xj, yj, zj, uj, vj, wj, pj, volume = [packed[place, field:field + 1, :] for field in range(8)]
            gap_x = xi - xj
            gap_y = yi - yj
            gap_z = zi - zj
            shifted = (gap_x * gap_x + eta_square) + (gap_y * gap_y + gap_z * gap_z)
            inv = lax.rsqrt(shifted)
            bump = jnp.maximum(2.0 - shifted * inv, 0.0)
            weight = (bump * bump) * (bump * volume)
            closing = (ui - uj) * gap_x + (vi - vj) * gap_y + (wi - wj) * gap_z
            inv_sq = inv * inv
            diff = weight * (pj - pi)
            push = weight * ((pi + pj) - closing * inv_sq)
            return (
                s_close + weight * closing,
                s_diff + diff,
                s_damp + diff * inv_sq,
                s_x + push * gap_x,
                s_y + push * gap_y,
                s_z + push * gap_z,
            )

        sums = (jnp.zeros((rows_step, slots), jnp.float32),) * 6
        def some_tiles(step, begin):
            def body(turn, sums):
                for more in range(step):
                    sums = one_tile(begin + turn * step + more, sums)
                return sums
            return body

        turns = (tiles + tail_step - 1) // main_step
        begin = turns * main_step
        tails = (jnp.maximum(tiles - begin, 0) + tail_step - 1) // tail_step
        sums = lax.fori_loop(0, turns, some_tiles(main_step, 0), sums)
        sums = lax.fori_loop(0, tails, some_tiles(tail_step, begin), sums)
        kept = (sums[0], sums[1] - eta_square * sums[2], sums[3], sums[4], sums[5])
        for which in range(5):
            totals[pl.ds(pl.multiple_of(which * slots + first, rows_step), rows_step), :] = kept[which]
        return unused

    lax.fori_loop(0, (live + rows_step - 1) // rows_step, per_rows, 0)

    @pl.when(block == blocks - 1)
    def _():
        finish(block)


def per_device(particles, counts, pairs):
    blocks, width, slots = particles.shape
    slab_blk = blocks * lax.axis_size("cross")
    cells_z = slab_blk // GY
    per_block = pairs.shape[1]
    vmem = pl.BlockSpec(memory_space=pltpu.VMEM)
    smem = pl.BlockSpec(memory_space=pltpu.SMEM)
    limit = pltpu.CompilerParams(vmem_limit_bytes=40 * 1024 * 1024)
    ready = pl.pallas_call(
        ready_kernel,
        out_shape=jax.ShapeDtypeStruct(particles.shape, jnp.float32),
        in_specs=[smem, vmem],
        out_specs=vmem,
        compiler_params=limit,
        name="ready",
    )(counts, particles)
    nearby = {offset: passed_along(ready, "flow", -offset) for offset in (-2, 2, -1)}
    spread = jnp.broadcast_to(ready[:, :fields, :, None], (blocks, fields, slots, slots))
    spread, held = lax.optimization_barrier((spread, ready))
    nearby[1] = passed_along(held, "flow", -1)
    listed = in_order(pairs)
    per_slab = per_block // len(slab_order)
    middle = per_slab * (len(slab_order) // 2)
    own_codes = listed[:, middle:middle + per_slab] - 2 * slab_blk
    far_codes = jnp.concatenate([listed[:, :middle], listed[:, middle + per_slab:] - slab_blk], axis=1)
    own_lookup = lax.all_gather(ready, "cross", axis=0, tiled=True)
    stacked = jnp.stack([nearby[offset] for offset in slab_order if offset])
    stacked, own_lookup = lax.optimization_barrier((stacked, own_lookup))
    far_lookup = lax.all_gather(stacked, "cross", axis=1, tiled=True)
    far_lookup = far_lookup.reshape((4 * slab_blk, width, slots))


    def rates(main_step, slabs, codes, lookup, more, name):
        slot_ids = jnp.arange(slots, dtype=jnp.int32)
        source_counts = jnp.max(jnp.where(lookup[:, 7] > 0.0, slot_ids[None, :] + 1, 0), axis=1)
        work = blocks * slots * slots * len(slabs) * per_slab
        return pl.pallas_call(
            functools.partial(pair_kernel, main_step, slabs, per_slab, 2.0 * GY, 2.0 * cells_z),
            out_shape=jax.ShapeDtypeStruct((blocks, 4, slots), jnp.float32),
            grid=(blocks,),
            in_specs=[smem, smem, smem, vmem, vmem]
            + [pl.BlockSpec((1, 1, slots, slots), lambda i, field=field: (i, field, 0, 0)) for field in range(fields)]
            + [vmem] * (len(more) + 1),
            out_specs=vmem,
            scratch_shapes=[
                pltpu.VMEM((len(slabs) * per_slab + main_step + tail_step, 8, slots), jnp.float32),
                pltpu.VMEM((5 * slots, slots), jnp.float32),
            ],
            compiler_params=limit,
            cost_estimate=pl.CostEstimate(flops=60 * work, bytes_accessed=4 * lookup.size, transcendentals=work),
            name=name,
        )(codes.reshape(-1), counts, source_counts, ready, lookup, *(fields * [spread]), *more, particles)

    own_rates = rates(8, (0.0,), own_codes, own_lookup, (), "own_slab")
    far_slabs = tuple(float(offset) for offset in slab_order if offset)
    return rates(12, far_slabs, far_codes, far_lookup, (own_rates,), "other_slabs")


def solution(mesh):
    placed = (P(("flow", "cross"), None, None), P(("flow", "cross")), P(("flow", "cross"), None))
    return jax.shard_map(
        per_device,
        mesh=mesh,
        in_specs=placed,
        out_specs=P(("flow", "cross"), None, None),
        check_vma=False,
    )
```

```python
import functools
import math

import jax
import jax.numpy as jnp
from jax import lax
from jax.experimental import pallas as pl
from jax.experimental.pallas import tpu as pltpu
from jax.sharding import PartitionSpec as P

GY = 8


kernel_coef = 5.0 * 21.0 / (16.0 * math.pi)
eta_square = 0.01
sound_speed = 6.0
delta_coef = 0.1
visc_coef = 0.1
slab_order = (-2, -1, 0, 1, 2)
wave = sound_speed * visc_coef
stiff = sound_speed / visc_coef
rows_step = 16
tail_step = 4
fields = 7


def passed_along(value, axis, steps):
    count = lax.axis_size(axis)
    pairs = [(source, (source + steps) % count) for source in range(count)]
    return lax.ppermute(value, axis, pairs)


def in_order(codes):
    places = jnp.arange(codes.shape[1], dtype=jnp.int32)
    mine, other = codes[:, :, None], codes[:, None, :]
    before = (other < mine) | ((other == mine) & (places[None, None, :] < places[None, :, None]))
    rank = jnp.sum(before.astype(jnp.int32), axis=2)
    return jnp.sum(jnp.where(rank[:, None, :] == places[None, :, None], codes[:, None, :], 0), axis=2)


def ready_kernel(counts, particles, out):
    blocks, width, slots = particles.shape
    lanes = lax.broadcasted_iota(jnp.int32, (1, slots), 1)

    def one(block, unused):
        rho = particles[block, 6:7, :]
        out[block, 0:6, :] = particles[block, 0:6, :]
        out[block, 6:7, :] = stiff * (rho - 1.0)
        out[block, 7:8, :] = jnp.where(lanes < counts[block], particles[block, 7:8, :] / rho, 0.0)
        return unused

    lax.fori_loop(0, blocks, one, 0, unroll=8)


def pair_kernel(main_step, slabs, per_slab, wide_y, wide_z, codes, live_counts, source_counts, ready, lookup, *rest_refs):
    spread, rest_refs = rest_refs[:fields], rest_refs[fields:]
    earlier = rest_refs[0] if len(rest_refs) == 5 else None
    particles, out, packed, totals = rest_refs[-4:]
    block = pl.program_id(0)
    blocks, width, slots = ready.shape
    lanes = lax.broadcasted_iota(jnp.int32, (8, slots), 1)
    row = lax.broadcasted_iota(jnp.int32, (8, slots), 0)
    wide = jnp.where(row == 1, wide_y, jnp.where(row == 2, wide_z, 0.0))
    inverse = jnp.where(row == 1, 1.0 / wide_y, jnp.where(row == 2, 1.0 / wide_z, 0.0))
    along = jnp.where(row == 0, 1.0, 0.0)
    empty = jnp.zeros((8, slots), jnp.float32)
    scale = kernel_coef / 8.0
    def finish(block):
        every = totals[...]
        high = every.astype(jnp.bfloat16)
        low = (every - high.astype(jnp.float32)).astype(jnp.bfloat16)
        ones = jnp.ones((2 * slots, slots), jnp.bfloat16)
        every = jnp.dot(jnp.concatenate([high, low], axis=1), ones, preferred_element_type=jnp.float32)
        rows = []
        for which in range(5):
            total = empty
            for group in range(slots // 8):
                begin = which * slots + group * 8
                total = total + jnp.where(lanes == row + group * 8, every[begin:begin + 8], 0.0)
            rows.append(jnp.sum(total, axis=0, keepdims=True))
        rho = particles[block, 6:7, :]
        drho = scale * (2.0 * delta_coef * sound_speed / stiff * rows[1] - rho * rows[0])
        over = (scale * wave) / rho
        alive = lanes[0:1] < live_counts[block]
        results = [drho] + [over * rows[2 + axis] for axis in range(3)]
        for place, result in enumerate(results):
            if earlier is not None:
                result = result + earlier[block, place:place + 1, :]
            out[block, place:place + 1, :] = jnp.where(alive, result, 0.0)

    finish(jnp.maximum(block - 1, 0))
    own = ready[block]
    own_first = jnp.broadcast_to(own[:, 0:1], (8, slots)) * inverse + 0.5

    current, tile, start = empty, jnp.int32(0), jnp.int32(0)
    shifts = []
    for step in range(len(slabs) * per_slab):
        slab, cell = divmod(step, per_slab)
        code = codes[block * (len(slabs) * per_slab) + step]
        count = source_counts[code]
        value = lookup[code]
        if slab == 0:
            first = jnp.broadcast_to(value[:, 0:1], (8, slots))
            shifts.append(wide * jnp.floor(own_first - first * inverse))
        value = value + (shifts[cell] + along * slabs[slab])
        turned = pltpu.roll(value, start, 1)
        ahead = lanes >= start
        merged = jnp.where(ahead, turned, current)
        packed[tile] = merged
        end = start + count
        full = (end >= slots).astype(jnp.int32)
        keep = jnp.broadcast_to(full, (8, slots)) == 0
        rest = jnp.where(ahead, 0.0, turned)
        current = jnp.where(keep, merged, rest)
        tile = tile + full
        start = end - full * slots
    packed[tile] = current
    for more in range(1, tail_step):
        packed[tile + more] = empty
    tiles = tile + (start > 0).astype(jnp.int32)
    live = live_counts[block]

    def per_rows(index, unused):
        first = pl.multiple_of(index * rows_step, rows_step)
        rows = pl.ds(first, rows_step)
        xi, yi, zi, ui, vi, wi, pi = [spread[field][0, 0, rows, :] for field in range(fields)]

        def one_tile(place, sums):
            s_close, s_diff, s_damp, s_x, s_y, s_z = sums
            xj, yj, zj, uj, vj, wj, pj, volume = [packed[place, field:field + 1, :] for field in range(8)]
            gap_x = xi - xj
            gap_y = yi - yj
            gap_z = zi - zj
            shifted = (gap_x * gap_x + eta_square) + (gap_y * gap_y + gap_z * gap_z)
            inv = lax.rsqrt(shifted)
            bump = jnp.maximum(2.0 - shifted * inv, 0.0)
            weight = (bump * bump) * (bump * volume)
            closing = (ui - uj) * gap_x + (vi - vj) * gap_y + (wi - wj) * gap_z
            inv_sq = inv * inv
            diff = weight * (pj - pi)
            push = weight * ((pi + pj) - closing * inv_sq)
            return (
                s_close + weight * closing,
                s_diff + diff,
                s_damp + diff * inv_sq,
                s_x + push * gap_x,
                s_y + push * gap_y,
                s_z + push * gap_z,
            )

        sums = (jnp.zeros((rows_step, slots), jnp.float32),) * 6
        def some_tiles(step, begin):
            def body(turn, sums):
                for more in range(step):
                    sums = one_tile(begin + turn * step + more, sums)
                return sums
            return body

        turns = (tiles + tail_step - 1) // main_step
        begin = turns * main_step
        tails = (jnp.maximum(tiles - begin, 0) + tail_step - 1) // tail_step
        sums = lax.fori_loop(0, turns, some_tiles(main_step, 0), sums)
        sums = lax.fori_loop(0, tails, some_tiles(tail_step, begin), sums)
        kept = (sums[0], sums[1] - eta_square * sums[2], sums[3], sums[4], sums[5])
        for which in range(5):
            totals[pl.ds(pl.multiple_of(which * slots + first, rows_step), rows_step), :] = kept[which]
        return unused

    lax.fori_loop(0, (live + rows_step - 1) // rows_step, per_rows, 0)

    @pl.when(block == blocks - 1)
    def _():
        finish(block)


def per_device(particles, counts, pairs):
    blocks, width, slots = particles.shape
    slab_blk = blocks * lax.axis_size("cross")
    cells_z = slab_blk // GY
    per_block = pairs.shape[1]
    vmem = pl.BlockSpec(memory_space=pltpu.VMEM)
    smem = pl.BlockSpec(memory_space=pltpu.SMEM)
    limit = pltpu.CompilerParams(vmem_limit_bytes=40 * 1024 * 1024)
    ready = pl.pallas_call(
        ready_kernel,
        out_shape=jax.ShapeDtypeStruct(particles.shape, jnp.float32),
        in_specs=[smem, vmem],
        out_specs=vmem,
        compiler_params=limit,
        name="ready",
    )(counts, particles)
    nearby = {offset: passed_along(ready, "flow", -offset) for offset in (-2, 2, -1)}
    spread = jnp.broadcast_to(ready[:, :fields, :, None], (blocks, fields, slots, slots))
    spread, held = lax.optimization_barrier((spread, ready))
    nearby[1] = passed_along(held, "flow", -1)
    listed = in_order(pairs)
    per_slab = per_block // len(slab_order)
    nearby[0] = ready
    stacked = jnp.stack([nearby[offset] for offset in slab_order])
    everyone = lax.all_gather(stacked, "cross", axis=1, tiled=True)
    everyone = everyone.reshape((len(slab_order) * slab_blk, width, slots))

    def rates(main_step, slabs, codes, lookup, more, name):
        slot_ids = jnp.arange(slots, dtype=jnp.int32)
        source_counts = jnp.max(jnp.where(lookup[:, 7] > 0.0, slot_ids[None, :] + 1, 0), axis=1)
        work = blocks * slots * slots * len(slabs) * per_slab
        return pl.pallas_call(
            functools.partial(pair_kernel, main_step, slabs, per_slab, 2.0 * GY, 2.0 * cells_z),
            out_shape=jax.ShapeDtypeStruct((blocks, 4, slots), jnp.float32),
            grid=(blocks,),
            in_specs=[smem, smem, smem, vmem, vmem]
            + [pl.BlockSpec((1, 1, slots, slots), lambda i, field=field: (i, field, 0, 0)) for field in range(fields)]
            + [vmem] * (len(more) + 1),
            out_specs=vmem,
            scratch_shapes=[
                pltpu.VMEM((len(slabs) * per_slab + main_step + tail_step, 8, slots), jnp.float32),
                pltpu.VMEM((5 * slots, slots), jnp.float32),
            ],
            compiler_params=limit,
            cost_estimate=pl.CostEstimate(flops=60 * work, bytes_accessed=4 * lookup.size, transcendentals=work),
            name=name,
        )(codes.reshape(-1), counts, source_counts, ready, lookup, *(fields * [spread]), *more, particles)

    return rates(12, tuple(float(offset) for offset in slab_order), listed, everyone, (), "all_slabs")


def solution(mesh):
    placed = (P(("flow", "cross"), None, None), P(("flow", "cross")), P(("flow", "cross"), None))
    return jax.shard_map(
        per_device,
        mesh=mesh,
        in_specs=placed,
        out_specs=P(("flow", "cross"), None, None),
        check_vma=False,
    )
```
